32 devices in a mesh: dp: 16 (over z, x, core), mp: 2 (over y).
Axes of the slice: x: 2, y: 2, z: 4, core: 2. Of those that a mesh axis runs over, the one named last changes fastest.
Arguments:
- inputs: bfloat16 [256, 6144], P('dp', 'mp'), may hold values from -6 to 6
- targets: bfloat16 [256, 6144], P('dp', 'mp'), may hold values from -6 to 6
- w_in: bfloat16 [6144, 16384], P('mp', 'dp'), may hold values from -6 to 6
- w_out: bfloat16 [16384, 6144], P('dp', 'mp'), may hold values from -6 to 6
- teach_in: float32 [6144, 16384], P('mp', 'dp'), may hold values from -6 to 6
- teach_out: float32 [16384, 6144], P('dp', 'mp'), may hold values from -6 to 6
Outputs:
- grad_in: bfloat16 [6144, 16384], P('mp', 'dp')
- grad_out: bfloat16 [16384, 6144], P('dp', 'mp')
- new_in: float32 [6144, 16384], P('mp', 'dp')
- new_out: float32 [16384, 6144], P('dp', 'mp')
The draws below stay inside these ranges and needn't reach their ends.
All inputs are finite; a program needn't handle non-finite values.
Results may differ from the reference program's by a relative error of at most 0.017.
Values may be sent and summed in bfloat16 or wider, within the bound.
A program may use at most 192 MiB of HBM per device.

```python
import math
import jax
import jax.numpy as jnp

D = 6144
FF = 16384
TOKENS = 256


def block_levels(own_key, dims, shards, smallest, high):
    factor_of, own = 1.0, jax.random.fold_in(own_key, 6)
    for dim, blocks in shards:
        heights = jnp.exp(jax.random.uniform(jax.random.fold_in(own, dim), (blocks,), jnp.float32, smallest / len(shards), high / len(shards)))
        factor_of = factor_of * jnp.repeat(heights, dims[dim] // blocks).reshape([-1 if axis == dim else 1 for axis in range(len(dims))])
    return factor_of


def normal_values(key, dims, deviation, reach, shards=(), kind=jnp.bfloat16):
    values = jax.random.normal(key, dims, jnp.float32) * deviation
    if len(shards) > 0:
        values = block_levels(key, dims, shards, -0.22, 0.18) * values
    return jnp.clip(values, min=-reach, max=reach).astype(kind)


def setup_inputs(seed: int = 0) -> dict:
    arg_keys = jax.random.split(jax.random.key(seed), 7)
    inputs = normal_values(arg_keys[0], (TOKENS, D), 1.0, 6.0, ((0, 16), (1, 2)))
    targets = normal_values(arg_keys[1], (TOKENS, D), 1.0, 6.0, ((0, 16), (1, 2)))
    w_in = normal_values(arg_keys[2], (D, FF), 1.0, 6.0, ((0, 2), (1, 16)))
    w_out = normal_values(arg_keys[3], (FF, D), 1.0, 6.0, ((0, 16), (1, 2)))
    teach_in = normal_values(arg_keys[4], (D, FF), 1.0, 6.0, ((0, 2), (1, 16)), jnp.float32)
    teach_out = normal_values(arg_keys[5], (FF, D), 1.0, 6.0, ((0, 16), (1, 2)), jnp.float32)
    return dict(inputs=inputs, targets=targets, w_in=w_in, w_out=w_out, teach_in=teach_in, teach_out=teach_out)


decay_rate = 0.99
step_size = 0.5

def gelu_value(value):
    return 0.5 * value * (1.0 + jax.scipy.special.erf(value * (1.0 / math.sqrt(2.0))))

def gelu_slope(value):
    normal_cdf = 0.5 * (1.0 + jax.scipy.special.erf(value * (1.0 / math.sqrt(2.0))))
    return normal_cdf + value * jnp.exp(-0.5 * value * value) * (1.0 / math.sqrt(2.0 * math.pi))

def reference(inputs, targets, w_in, w_out, teach_in, teach_out):
    in_scale = 1.0 / math.sqrt(D)
    out_scale = 1.0 / math.sqrt(FF)
    preact = jnp.dot(inputs, w_in, preferred_element_type=jnp.float32) * in_scale
    hidden = gelu_value(preact).astype(jnp.bfloat16)
    outputs = inputs.astype(jnp.float32) + jnp.dot(hidden, w_out, preferred_element_type=jnp.float32) * out_scale
    slope = (outputs - targets.astype(jnp.float32)).astype(jnp.bfloat16)
    grad_out = jnp.dot(hidden.T, slope, preferred_element_type=jnp.float32) * out_scale
    hidden_slope = jnp.dot(slope, w_out.T, preferred_element_type=jnp.float32) * out_scale
    pre_slope = (hidden_slope * gelu_slope(preact)).astype(jnp.bfloat16)
    grad_in = jnp.dot(inputs.T, pre_slope, preferred_element_type=jnp.float32) * in_scale
    new_in = decay_rate * teach_in + (1.0 - decay_rate) * (w_in.astype(jnp.float32) - step_size * grad_in)
    new_out = decay_rate * teach_out + (1.0 - decay_rate) * (w_out.astype(jnp.float32) - step_size * grad_out)
    return (grad_in.astype(jnp.bfloat16), grad_out.astype(jnp.bfloat16), new_in, new_out)
```

```python
import functools
import math

import jax
import jax.numpy as jnp
from jax import lax
from jax.experimental import pallas as pl
from jax.experimental.pallas import tpu as pltpu
from jax.sharding import PartitionSpec as P

decay_rate = 0.99
step_size = 0.5
MESH = pl.DeviceIdType.MESH
F32 = jnp.float32
BF16 = jnp.bfloat16
MIB = 1024 * 1024


def normal_cdf(value):
    return 0.5 * (1.0 + lax.erf(value * (1.0 / math.sqrt(2.0))))


def gelu_slope(value, cdf):
    return cdf + value * jnp.exp(-0.5 * value * value) * (1.0 / math.sqrt(2.0 * math.pi))


def forward_kernel(
    nz, in_scale, out_scale,
    x_ref, t_ref, w_in_hbm, w_out_hbm,
    g_hbm, h_hbm, s_hbm, part_hbm, gs_hbm,
    w_in, w_out, g, s, pre_send, pre_recv, pre, h, part, acc, own,
    c_out, c_in, x_out, x_in, z_out, z_in,
    w_sem, o_sem,
    ag_recv, ag_zs, ag_xs, ag_cs,
    sg_recv, sg_zs, sg_xs, sg_cs,
    y_s, y_r, c_s, c_r, x_s, x_r, z_s, z_r,
):
    rows, feats = x_ref.shape
    ff = w_in.shape[1]
    group = 4 * rows
    chunk = 2 * group
    me = lax.axis_index("dp")
    my = lax.axis_index("mp")
    z, xc = me // 4, me % 4
    x, c = xc // 2, xc % 2
    ox, oc = 1 - x, 1 - c

    def index(zi, xi, ci):
        return (zi * 2 + xi) * 2 + ci

    def z_of(k):
        return ((z // 2 + k // 2) % (nz // 2)) * 2 + (z % 2 + k % 2) % 2

    loads = [
        pltpu.make_async_copy(w_in_hbm, w_in, w_sem.at[0]),
        pltpu.make_async_copy(w_out_hbm, w_out, w_sem.at[1]),
    ]
    for load in loads:
        load.start()

    barrier = pltpu.get_barrier_semaphore()
    for k in range(1, nz):
        pl.semaphore_signal(barrier, inc=1, device_id={"dp": index(z_of(k), x, c)}, device_id_type=MESH)
    pl.semaphore_signal(barrier, inc=1, device_id={"dp": index(z, ox, c)}, device_id_type=MESH)
    pl.semaphore_signal(barrier, inc=1, device_id={"dp": index(z, x, oc)}, device_id_type=MESH)
    pl.semaphore_signal(barrier, inc=1, device_id={"mp": 1 - my}, device_id_type=MESH)
    pl.semaphore_wait(barrier, nz + 2)

    def send(src, dst, ssem, rsem, to):
        copy = pltpu.make_async_remote_copy(
            src_ref=src, dst_ref=dst, send_sem=ssem, recv_sem=rsem,
            device_id=to, device_id_type=MESH,
        )
        return copy

    pending = []

    def go(copy):
        copy.start()
        pending.append(copy)

    def gather(buf, recv, zs, xs, cs):
        def shard(o):
            return buf.at[pl.ds(pl.multiple_of(o * rows, rows), rows), :]

        def move(o, ssem, to):
            return send(shard(o), shard(o), ssem, recv.at[o], {"dp": to})

        to_x, to_c = index(z, ox, c), index(z, x, oc)

        def begin():
            go(move(me, xs.at[0], to_x))
            for k in range(1, nz):
                go(move(me, zs.at[k], index(z_of(k), x, c)))
            go(move(me, cs.at[0], to_c))

        def z_arrive(k):
            o = index(z_of(k), x, c)
            move(o, zs.at[k], to_c).wait_recv()
            go(move(o, xs.at[k], to_x))
            go(move(o, cs.at[k], to_c))

        def x_arrive(k):
            o = index(z_of(k), ox, c)
            move(o, xs.at[k], to_c).wait_recv()
            go(move(o, cs.at[nz + k], to_c))

        def c_arrive(k):
            for xi in (x, ox):
                move(index(z_of(k), xi, oc), cs.at[k], to_c).wait_recv()

        def arrive(j):
            if j == 0:
                z_arrive(1)
                x_arrive(0)
                x_arrive(1)
                for k in range(2, nz):
                    z_arrive(k)
            else:
                x_arrive(2 * j)
                x_arrive(2 * j + 1)
            c_arrive(2 * j)
            c_arrive(2 * j + 1)

        return begin, arrive

    def chunk_rows(j):
        return pl.ds(pl.multiple_of((z_of(2 * j) // 2) * chunk, chunk), chunk)

    begin, arrive = gather(g, ag_recv, ag_zs, ag_xs, ag_cs)
    g[pl.ds(pl.multiple_of(me * rows, rows), rows), :] = x_ref[...]
    begin()

    def pre_step(j):
        arrive(j)
        if j == 0:
            loads[0].wait()
        at = chunk_rows(j)
        tile = 256

        @pl.loop(0, ff // tile)
        def _(i):
            cols = pl.ds(pl.multiple_of(i * tile, tile), tile)
            value = jnp.dot(g[at, :], w_in[:, cols], preferred_element_type=F32) * in_scale
            pre[at, cols] = value
            pre_send[at, cols] = value.astype(BF16)

        go(send(pre_send.at[at, :], pre_recv.at[at, :], y_s.at[j], y_r.at[j], {"mp": 1 - my}))

    def out_step(j):
        at = chunk_rows(j)
        send(pre_send.at[at, :], pre_recv.at[at, :], y_s.at[j], y_r.at[j], {"mp": 1 - my}).wait_recv()
        tile = 256

        @pl.loop(0, ff // tile)
        def _(i):
            cols = pl.ds(pl.multiple_of(i * tile, tile), tile)
            value = pre[at, cols] + pre_recv[at, cols].astype(F32)
            cdf = normal_cdf(value)
            h[at, cols] = (value * cdf).astype(BF16)
            pre[at, cols] = gelu_slope(value, cdf)

        if j == 0:
            loads[1].wait()

        @pl.loop(0, feats // tile)
        def _(i):
            cols = pl.ds(pl.multiple_of(i * tile, tile), tile)
            acc[at, cols] = jnp.dot(h[at, :], w_out[:, cols], preferred_element_type=F32) * out_scale

        for k in (2 * j, 2 * j + 1):
            for xi in range(2):
                src = pl.ds(pl.multiple_of(index(z_of(k), xi, oc) * rows, rows), rows)
                c_out[k, pl.ds(xi * rows, rows), :] = acc[src, :].astype(BF16)
            go(send(c_out.at[k], c_in.at[k], c_s.at[k], c_r.at[k], {"dp": index(z, x, oc)}))

    def core_step(k):
        send(c_out.at[k], c_in.at[k], c_s.at[k], c_r.at[k], {"dp": index(z, x, oc)}).wait_recv()

        def total(xi):
            src = pl.ds(pl.multiple_of(index(z_of(k), xi, c) * rows, rows), rows)
            return acc[src, :] + c_in[k, pl.ds(pl.multiple_of(xi * rows, rows), rows), :].astype(F32)

        x_out[k] = total(ox).astype(BF16)
        go(send(x_out.at[k], x_in.at[k], x_s.at[k], x_r.at[k], {"dp": index(z, ox, c)}))
        own[k] = total(x)

    def x_step(k):
        send(x_out.at[k], x_in.at[k], x_s.at[k], x_r.at[k], {"dp": index(z, ox, c)}).wait_recv()
        value = own[k] + x_in[k].astype(F32)
        if k == 0:
            own[k] = value
        else:
            z_out[k] = value.astype(BF16)
            go(send(z_out.at[k], z_in.at[z], z_s.at[k], z_r.at[z], {"dp": index(z_of(k), x, c)}))

    outs = []

    def store(src, dst, i):
        copy = pltpu.make_async_copy(src, dst, o_sem.at[i])
        copy.start()
        outs.append(copy)

    chunks = nz // 2
    for j in range(chunks):
        pre_step(j)
    store(g, g_hbm, 0)
    for j in range(chunks):
        out_step(j)
        if j > 0:
            x_step(2 * j - 2)
            x_step(2 * j - 1)
        core_step(2 * j)
        core_step(2 * j + 1)
    x_step(nz - 2)
    x_step(nz - 1)
    store(h, h_hbm, 1)
    store(pre, gs_hbm, 2)

    begin, arrive = gather(s, sg_recv, sg_zs, sg_xs, sg_cs)
    summed = own[0]
    for k in range(1, nz):
        zi = z_of(k)
        send(z_out.at[k], z_in.at[zi], z_s.at[k], z_r.at[zi], {"dp": index(zi, x, c)}).wait_recv()
        summed += z_in[zi].astype(F32)
    slope = x_ref[...].astype(F32) + summed - t_ref[...].astype(F32)
    s[pl.ds(pl.multiple_of(me * rows, rows), rows), :] = slope.astype(BF16)
    begin()

    for j in range(chunks):
        arrive(j)
        at = chunk_rows(j)
        tile = 256

        @pl.loop(0, ff // tile)
        def _(i):
            units = pl.ds(pl.multiple_of(i * tile, tile), tile)
            value = lax.dot_general(
                s[at, :], w_out[units, :], (((1,), (1,)), ((), ())), preferred_element_type=F32
            )
            part[at, units] = (value * out_scale).astype(BF16)

    store(s, s_hbm, 3)
    store(part, part_hbm, 4)
    for copy in pending:
        copy.wait_send()
    for copy in outs:
        copy.wait()


def forward(nz, in_scale, out_scale, inputs, targets, w_in, w_out):
    rows, feats = inputs.shape
    ff = w_in.shape[1]
    tokens = rows * nz * 4
    dma = pltpu.SemaphoreType.DMA
    vmem = pl.BlockSpec(memory_space=pltpu.VMEM)
    anywhere = pl.BlockSpec(memory_space=pl.ANY)
    return pl.pallas_call(
        functools.partial(forward_kernel, nz, in_scale, out_scale),
        out_shape=(
            jax.ShapeDtypeStruct((tokens, feats), BF16),
            jax.ShapeDtypeStruct((tokens, ff), BF16),
            jax.ShapeDtypeStruct((tokens, feats), BF16),
            jax.ShapeDtypeStruct((tokens, ff), BF16),
            jax.ShapeDtypeStruct((tokens, ff), F32),
        ),
        in_specs=[vmem, vmem, anywhere, anywhere],
        out_specs=(anywhere,) * 5,
        scratch_shapes=[
            pltpu.VMEM((feats, ff), BF16),
            pltpu.VMEM((ff, feats), BF16),
            pltpu.VMEM((tokens, feats), BF16),
            pltpu.VMEM((tokens, feats), BF16),
            pltpu.VMEM((tokens, ff), BF16),
            pltpu.VMEM((tokens, ff), BF16),
            pltpu.VMEM((tokens, ff), F32),
            pltpu.VMEM((tokens, ff), BF16),
            pltpu.VMEM((tokens, ff), BF16),
            pltpu.VMEM((tokens, feats), F32),
            pltpu.VMEM((nz, rows, feats), F32),
            pltpu.VMEM((nz, 2 * rows, feats), BF16),
            pltpu.VMEM((nz, 2 * rows, feats), BF16),
            pltpu.VMEM((nz, rows, feats), BF16),
            pltpu.VMEM((nz, rows, feats), BF16),
            pltpu.VMEM((nz, rows, feats), BF16),
            pltpu.VMEM((nz, rows, feats), BF16),
            dma((2,)), dma((5,)),
            dma((4 * nz,)), dma((nz,)), dma((nz,)), dma((2 * nz,)),
            dma((4 * nz,)), dma((nz,)), dma((nz,)), dma((2 * nz,)),
            dma((nz // 2,)), dma((nz // 2,)),
            dma((nz,)), dma((nz,)), dma((nz,)), dma((nz,)), dma((nz,)), dma((nz,)),
        ],
        compiler_params=pltpu.CompilerParams(
            collective_id=0, has_side_effects=True, vmem_limit_bytes=48 * MIB
        ),
        cost_estimate=pl.CostEstimate(
            flops=6 * tokens * feats * ff, bytes_accessed=6 * feats * ff, transcendentals=0
        ),
        name="forward",
    )(inputs, targets, w_in, w_out)


def blended(teach, weight, grad):
    return decay_rate * teach + (1.0 - decay_rate) * (weight.astype(F32) - step_size * grad)


def out_kernel(scale, h_ref, s_ref, w_ref, t_ref, grad_ref, new_ref):
    grad = lax.dot_general(
        h_ref[...], s_ref[...], (((0,), (0,)), ((), ())), preferred_element_type=F32
    ) * scale
    grad_ref[...] = grad.astype(BF16)
    new_ref[...] = blended(t_ref[...], w_ref[...], grad)


def update_out(scale, hidden, slope, w_out, teach_out):
    ff, feats = w_out.shape
    tokens = hidden.shape[0]
    tile = 128
    row_block = pl.BlockSpec((tile, feats), lambda i: (i, 0))
    return pl.pallas_call(
        functools.partial(out_kernel, scale),
        grid=(ff // tile,),
        out_shape=(jax.ShapeDtypeStruct((ff, feats), BF16), jax.ShapeDtypeStruct((ff, feats), F32)),
        in_specs=[
            pl.BlockSpec((tokens, tile), lambda i: (0, i)),
            pl.BlockSpec((tokens, feats), lambda i: (0, 0)),
            row_block,
            row_block,
        ],
        out_specs=(row_block, row_block),
        compiler_params=pltpu.CompilerParams(vmem_limit_bytes=40 * MIB),
        cost_estimate=pl.CostEstimate(
            flops=2 * tokens * feats * ff, bytes_accessed=12 * feats * ff, transcendentals=0
        ),
        name="update_out",
    )(hidden, slope, w_out, teach_out)


def in_kernel(scale, g_ref, part_ref, other_ref, gs_ref, w_ref, t_ref, grad_ref, new_ref, pre_slope):
    @pl.when(pl.program_id(0) == 0)
    def _():
        total = part_ref[...].astype(F32) + other_ref[...].astype(F32)
        pre_slope[...] = (total * gs_ref[...]).astype(BF16)

    grad = lax.dot_general(
        g_ref[...], pre_slope[...], (((0,), (0,)), ((), ())), preferred_element_type=F32
    ) * scale
    grad_ref[...] = grad.astype(BF16)
    new_ref[...] = blended(t_ref[...], w_ref[...], grad)


def update_in(scale, gathered, part, other, gs, w_in, teach_in):
    feats, ff = w_in.shape
    tokens = gathered.shape[0]
    tile = 384 if feats % 384 == 0 else 128
    row_block = pl.BlockSpec((tile, ff), lambda i: (i, 0))
    whole = pl.BlockSpec((tokens, ff), lambda i: (0, 0))
    return pl.pallas_call(
        functools.partial(in_kernel, scale),
        grid=(feats // tile,),
        out_shape=(jax.ShapeDtypeStruct((feats, ff), BF16), jax.ShapeDtypeStruct((feats, ff), F32)),
        in_specs=[
            pl.BlockSpec((tokens, tile), lambda i: (0, i)),
            whole, whole, whole,
            row_block,
            row_block,
        ],
        out_specs=(row_block, row_block),
        scratch_shapes=[pltpu.VMEM((tokens, ff), BF16)],
        compiler_params=pltpu.CompilerParams(vmem_limit_bytes=40 * MIB),
        cost_estimate=pl.CostEstimate(
            flops=2 * tokens * feats * ff, bytes_accessed=12 * feats * ff, transcendentals=0
        ),
        name="update_in",
    )(gathered, part, other, gs, w_in, teach_in)


def shards(dp, mp, inputs, targets, w_in, w_out, teach_in, teach_out):
    in_scale = 1.0 / math.sqrt(inputs.shape[1] * mp)
    out_scale = 1.0 / math.sqrt(w_out.shape[0] * dp)
    gathered, hidden, slope, part, gs = forward(
        dp // 4, in_scale, out_scale, inputs, targets, w_in, w_out
    )
    other = lax.ppermute(part, "mp", [(0, 1), (1, 0)])
    grad_out, new_out = update_out(out_scale, hidden, slope, w_out, teach_out)
    grad_in, new_in = update_in(in_scale, gathered, part, other, gs, w_in, teach_in)
    return grad_in, grad_out, new_in, new_out


def plain_shards(dp, mp, inputs, targets, w_in, w_out, teach_in, teach_out):
    in_scale = 1.0 / math.sqrt(inputs.shape[1] * mp)
    out_scale = 1.0 / math.sqrt(w_out.shape[0] * dp)
    gathered = lax.all_gather(inputs, "dp", axis=0, tiled=True)
    preact = lax.psum(jnp.dot(gathered, w_in, preferred_element_type=F32) * in_scale, "mp")
    cdf = normal_cdf(preact)
    hidden = (preact * cdf).astype(BF16)
    summed = lax.psum_scatter(
        jnp.dot(hidden, w_out, preferred_element_type=F32) * out_scale,
        "dp", scatter_dimension=0, tiled=True,
    )
    own = (inputs.astype(F32) + summed - targets.astype(F32)).astype(BF16)
    slope = lax.all_gather(own, "dp", axis=0, tiled=True)
    part = jnp.einsum("td,fd->tf", slope, w_out, preferred_element_type=F32) * out_scale
    hidden_slope = lax.psum(part.astype(BF16), "mp").astype(F32)
    pre_slope = (hidden_slope * gelu_slope(preact, cdf)).astype(BF16)
    g_out = jnp.einsum("tf,td->fd", hidden, slope, preferred_element_type=F32) * out_scale
    g_in = jnp.einsum("td,tf->df", gathered, pre_slope, preferred_element_type=F32) * in_scale
    new_in = blended(teach_in, w_in, g_in)
    new_out = blended(teach_out, w_out, g_out)
    return g_in.astype(BF16), g_out.astype(BF16), new_in, new_out


def solution(mesh):
    dp, mp = mesh.shape["dp"], mesh.shape["mp"]
    body = shards if mp == 2 and dp == 16 else plain_shards
    return jax.shard_map(
        functools.partial(body, dp, mp),
        mesh=mesh,
        in_specs=(
            P("dp", "mp"),
            P("dp", "mp"),
            P("mp", "dp"),
            P("dp", "mp"),
            P("mp", "dp"),
            P("dp", "mp"),
        ),
        out_specs=(P("mp", "dp"), P("dp", "mp"), P("mp", "dp"), P("dp", "mp")),
        check_vma=False,
    )
```

```python
import functools
import math

import jax
import jax.numpy as jnp
from jax import lax
from jax.experimental import pallas as pl
from jax.experimental.pallas import tpu as pltpu
from jax.sharding import PartitionSpec as P

decay_rate = 0.99
step_size = 0.5
MESH = pl.DeviceIdType.MESH
F32 = jnp.float32
BF16 = jnp.bfloat16
MIB = 1024 * 1024


def normal_cdf(value):
    return 0.5 * (1.0 + lax.erf(value * (1.0 / math.sqrt(2.0))))


def gelu_slope(value, cdf):
    return cdf + value * jnp.exp(-0.5 * value * value) * (1.0 / math.sqrt(2.0 * math.pi))


def blended(teach, weight, grad):
    return decay_rate * teach + (1.0 - decay_rate) * (weight.astype(F32) - step_size * grad)


def forward_kernel(
    nz, in_scale, out_scale,
    x_hbm, t_hbm, w_in_hbm, w_out_hbm, teach_out_hbm,
    g, h, s, part, pre, w_in, w_out, teach_out,
    t_own, pre_send, pre_recv, acc, own,
    c_out, c_in, x_out, x_in, z_out, z_in,
    w_sem,
    ag_recv, ag_zs, ag_xs, ag_cs,
    sg_recv, sg_zs, sg_xs, sg_cs,
    y_s, y_r, c_s, c_r, x_s, x_r, z_s, z_r,
):
    rows, feats = t_own.shape
    ff = w_in.shape[1]
    group = 4 * rows
    me = lax.axis_index("dp")
    my = lax.axis_index("mp")
    z, xc = me // 4, me % 4
    x, c = xc // 2, xc % 2
    ox, oc = 1 - x, 1 - c
    mine = pl.ds(pl.multiple_of(me * rows, rows), rows)

    def index(zi, xi, ci):
        return (zi * 2 + xi) * 2 + ci

    def z_of(k):
        return ((z // 2 + k // 2) % (nz // 2)) * 2 + (z % 2 + k % 2) % 2

    loads = [
        pltpu.make_async_copy(src, dst, w_sem.at[i])
        for i, (src, dst) in enumerate((
            (x_hbm, g.at[mine, :]), (t_hbm, t_own), (w_in_hbm, w_in),
            (w_out_hbm, w_out), (teach_out_hbm, teach_out),
        ))
    ]
    for load in loads[:3]:
        load.start()

    barrier = pltpu.get_barrier_semaphore()
    for k in range(1, nz):
        pl.semaphore_signal(barrier, inc=1, device_id={"dp": index(z_of(k), x, c)}, device_id_type=MESH)
    pl.semaphore_signal(barrier, inc=1, device_id={"dp": index(z, ox, c)}, device_id_type=MESH)
    pl.semaphore_signal(barrier, inc=1, device_id={"dp": index(z, x, oc)}, device_id_type=MESH)
    pl.semaphore_signal(barrier, inc=1, device_id={"mp": 1 - my}, device_id_type=MESH)
    pl.semaphore_wait(barrier, nz + 2)

    def send(src, dst, ssem, rsem, to):
        return pltpu.make_async_remote_copy(
            src_ref=src, dst_ref=dst, send_sem=ssem, recv_sem=rsem,
            device_id=to, device_id_type=MESH,
        )

    pending = []

    def go(copy):
        copy.start()
        pending.append(copy)

    def gather(buf, recv, zs, xs, cs):
        def shard(o):
            return buf.at[pl.ds(pl.multiple_of(o * rows, rows), rows), :]

        def move(o, ssem, to):
            return send(shard(o), shard(o), ssem, recv.at[o], {"dp": to})

        to_x, to_c = index(z, ox, c), index(z, x, oc)

        def begin():
            go(move(me, xs.at[0], to_x))
            for k in range(1, nz):
                go(move(me, zs.at[k], index(z_of(k), x, c)))
            go(move(me, cs.at[0], to_c))

        def z_arrive(k):
            o = index(z_of(k), x, c)
            move(o, zs.at[k], to_c).wait_recv()
            go(move(o, xs.at[k], to_x))
            go(move(o, cs.at[k], to_c))

        def x_arrive(k):
            o = index(z_of(k), ox, c)
            move(o, xs.at[k], to_c).wait_recv()
            go(move(o, cs.at[nz + k], to_c))

        def c_arrive(k):
            for xi in (x, ox):
                move(index(z_of(k), xi, oc), cs.at[k], to_c).wait_recv()

        return begin, z_arrive, x_arrive, c_arrive

    def group_rows(k):
        return pl.ds(pl.multiple_of(z_of(k) * group, group), group)

    def pair_rows(j):
        return pl.ds(pl.multiple_of((z_of(2 * j) // 2) * 2 * group, 2 * group), 2 * group)

    begin, z_arrive, x_arrive, c_arrive = gather(g, ag_recv, ag_zs, ag_xs, ag_cs)
    loads[0].wait()
    begin()
    for load in loads[3:]:
        load.start()

    def pre_step(k):
        x_arrive(k)
        c_arrive(k)
        if k == 0:
            loads[2].wait()
        at = group_rows(k)
        tile = 256

        @pl.loop(0, ff // tile)
        def _(i):
            cols = pl.ds(pl.multiple_of(i * tile, tile), tile)
            value = jnp.dot(g[at, :], w_in[:, cols], preferred_element_type=F32) * in_scale
            pre[at, cols] = value
            pre_send[at, cols] = value.astype(BF16)

        go(send(pre_send.at[at, :], pre_recv.at[at, :], y_s.at[k], y_r.at[k], {"mp": 1 - my}))

    def out_step(k):
        at = group_rows(k)
        send(pre_send.at[at, :], pre_recv.at[at, :], y_s.at[k], y_r.at[k], {"mp": 1 - my}).wait_recv()
        tile = 256

        @pl.loop(0, ff // tile)
        def _(i):
            cols = pl.ds(pl.multiple_of(i * tile, tile), tile)
            value = pre[at, cols] + pre_recv[at, cols].astype(F32)
            cdf = normal_cdf(value)
            h[at, cols] = (value * cdf).astype(BF16)
            pre[at, cols] = gelu_slope(value, cdf)

        if k == 0:
            loads[3].wait()

        @pl.loop(0, feats // tile)
        def _(i):
            cols = pl.ds(pl.multiple_of(i * tile, tile), tile)
            acc[at, cols] = jnp.dot(h[at, :], w_out[:, cols], preferred_element_type=F32) * out_scale

        for xi in range(2):
            src = pl.ds(pl.multiple_of(index(z_of(k), xi, oc) * rows, rows), rows)
            c_out[k, pl.ds(xi * rows, rows), :] = acc[src, :].astype(BF16)
        go(send(c_out.at[k], c_in.at[k], c_s.at[k], c_r.at[k], {"dp": index(z, x, oc)}))

    def core_step(k):
        send(c_out.at[k], c_in.at[k], c_s.at[k], c_r.at[k], {"dp": index(z, x, oc)}).wait_recv()

        def total(xi):
            src = pl.ds(pl.multiple_of(index(z_of(k), xi, c) * rows, rows), rows)
            return acc[src, :] + c_in[k, pl.ds(pl.multiple_of(xi * rows, rows), rows), :].astype(F32)

        x_out[k] = total(ox).astype(BF16)
        go(send(x_out.at[k], x_in.at[k], x_s.at[k], x_r.at[k], {"dp": index(z, ox, c)}))
        own[k] = total(x)

    def x_step(k):
        send(x_out.at[k], x_in.at[k], x_s.at[k], x_r.at[k], {"dp": index(z, ox, c)}).wait_recv()
        value = own[k] + x_in[k].astype(F32)
        if k == 0:
            own[k] = value
        else:
            z_out[k] = value.astype(BF16)
            go(send(z_out.at[k], z_in.at[z], z_s.at[k], z_r.at[z], {"dp": index(z_of(k), x, c)}))

    z_arrive(1)
    pre_step(0)
    pre_step(1)
    for k in range(2, nz):
        z_arrive(k)
    for k in range(nz):
        out_step(k)
        if k + 2 < nz:
            pre_step(k + 2)
        if k > 0:
            x_step(k - 1)
        core_step(k)
    x_step(nz - 1)

    begin, z_arrive, x_arrive, c_arrive = gather(s, sg_recv, sg_zs, sg_xs, sg_cs)
    loads[1].wait()
    summed = own[0]
    for k in range(1, nz):
        zi = z_of(k)
        send(z_out.at[k], z_in.at[zi], z_s.at[k], z_r.at[zi], {"dp": index(zi, x, c)}).wait_recv()
        summed += z_in[zi].astype(F32)
    slope = g[mine, :].astype(F32) + summed - t_own[...].astype(F32)
    s[mine, :] = slope.astype(BF16)
    begin()

    for j in range(nz // 2):
        if j == 0:
            z_arrive(1)
            x_arrive(0)
            x_arrive(1)
            for k in range(2, nz):
                z_arrive(k)
        else:
            x_arrive(2 * j)
            x_arrive(2 * j + 1)
        c_arrive(2 * j)
        c_arrive(2 * j + 1)
        at = pair_rows(j)
        tile = 256

        @pl.loop(0, ff // tile)
        def _(i):
            units = pl.ds(pl.multiple_of(i * tile, tile), tile)
            value = lax.dot_general(
                s[at, :], w_out[units, :], (((1,), (1,)), ((), ())), preferred_element_type=F32
            )
            part[at, units] = (value * out_scale).astype(BF16)

    for copy in pending:
        copy.wait_send()
    for load in loads[4:]:
        load.wait()


def forward(nz, in_scale, out_scale, inputs, targets, w_in, w_out, teach_out):
    rows, feats = inputs.shape
    ff = w_in.shape[1]
    tokens = rows * nz * 4
    dma = pltpu.SemaphoreType.DMA
    vmem = pl.BlockSpec(memory_space=pltpu.VMEM)
    return pl.pallas_call(
        functools.partial(forward_kernel, nz, in_scale, out_scale),
        out_shape=(
            pltpu.VMEM((tokens, feats), BF16),
            pltpu.VMEM((tokens, ff), BF16),
            pltpu.VMEM((tokens, feats), BF16),
            pltpu.VMEM((tokens, ff), BF16),
            pltpu.VMEM((tokens, ff), F32),
            pltpu.VMEM((feats, ff), BF16),
            pltpu.VMEM((ff, feats), BF16),
            pltpu.VMEM((ff, feats), F32),
        ),
        in_specs=[pl.BlockSpec(memory_space=pltpu.HBM)] * 5,
        out_specs=(vmem,) * 8,
        scratch_shapes=[
            pltpu.VMEM((rows, feats), BF16),
            pltpu.VMEM((tokens, ff), BF16),
            pltpu.VMEM((tokens, ff), BF16),
            pltpu.VMEM((tokens, feats), F32),
            pltpu.VMEM((nz, rows, feats), F32),
            pltpu.VMEM((nz, 2 * rows, feats), BF16),
            pltpu.VMEM((nz, 2 * rows, feats), BF16),
            pltpu.VMEM((nz, rows, feats), BF16),
            pltpu.VMEM((nz, rows, feats), BF16),
            pltpu.VMEM((nz, rows, feats), BF16),
            pltpu.VMEM((nz, rows, feats), BF16),
            dma((5,)),
            dma((4 * nz,)), dma((nz,)), dma((nz,)), dma((2 * nz,)),
            dma((4 * nz,)), dma((nz,)), dma((nz,)), dma((2 * nz,)),
            dma((nz,)), dma((nz,)),
            dma((nz,)), dma((nz,)), dma((nz,)), dma((nz,)), dma((nz,)), dma((nz,)),
        ],
        compiler_params=pltpu.CompilerParams(
            collective_id=0, has_side_effects=True, vmem_limit_bytes=12 * MIB
        ),
        cost_estimate=pl.CostEstimate(
            flops=6 * tokens * feats * ff, bytes_accessed=12 * feats * ff, transcendentals=0
        ),
        name="forward",
    )(*[
        pltpu.with_memory_space_constraint(x, pltpu.HBM)
        for x in (inputs, targets, w_in, w_out, teach_out)
    ])


def write_update(scale, tile, cols_tile, left, right, w, t, grad_hbm, new_hbm, grads, news, turned, sems):
    count, width = w.shape
    slots = grads.shape[0]
    copies = []
    for i in range(count // tile):
        slot = i % slots
        if i >= slots:
            for copy in copies[i - slots]:
                copy.wait()
        at = pl.ds(i * tile, tile)
        turned[...] = left[:, i * tile:(i + 1) * tile].T

        @pl.loop(0, width // cols_tile)
        def _(n):
            cols = pl.ds(pl.multiple_of(n * cols_tile, cols_tile), cols_tile)
            grad = jnp.dot(turned[...], right[:, cols], preferred_element_type=F32) * scale
            grads[slot, :, cols] = grad.astype(BF16)
            news[slot, :, cols] = blended(t[at, cols], w[at, cols], grad)

        pair = (
            pltpu.make_async_copy(grads.at[slot], grad_hbm.at[at, :], sems.at[0, slot]),
            pltpu.make_async_copy(news.at[slot], new_hbm.at[at, :], sems.at[1, slot]),
        )
        for copy in pair:
            copy.start()
        copies.append(pair)
    for pair in copies[-slots:]:
        for copy in pair:
            copy.wait()


def out_kernel(scale, tile, cols, h, s, w, t, *rest):
    write_update(scale, tile, cols, h, s, w, t, *rest)


def in_kernel(scale, tile, cols, g, part, other, gs, w, t, grad_hbm, new_hbm, grads, news, turned, sems, pre_slope):
    total = part[...].astype(F32) + other[...].astype(F32)
    pre_slope[...] = (total * gs[...]).astype(BF16)
    write_update(scale, tile, cols, g, pre_slope, w, t, grad_hbm, new_hbm, grads, news, turned, sems)


def update(kernel, name, scale, tile, cols, extra, tokens, *operands):
    count, width = operands[-1].shape
    slots = 3
    vmem = pl.BlockSpec(memory_space=pltpu.VMEM)
    anywhere = pl.BlockSpec(memory_space=pl.ANY)
    return pl.pallas_call(
        functools.partial(kernel, scale, tile, cols),
        out_shape=(
            jax.ShapeDtypeStruct((count, width), BF16),
            jax.ShapeDtypeStruct((count, width), F32),
        ),
        in_specs=[vmem] * len(operands),
        out_specs=(anywhere, anywhere),
        scratch_shapes=[
            pltpu.VMEM((slots, tile, width), BF16),
            pltpu.VMEM((slots, tile, width), F32),
            pltpu.VMEM((tile, tokens), BF16),
            pltpu.SemaphoreType.DMA((2, slots)),
            *extra,
        ],
        compiler_params=pltpu.CompilerParams(vmem_limit_bytes=12 * MIB),
        cost_estimate=pl.CostEstimate(
            flops=2 * tokens * count * width, bytes_accessed=12 * count * width, transcendentals=0
        ),
        name=name,
    )(*[pltpu.with_memory_space_constraint(x, pltpu.VMEM) for x in operands])


def shards(dp, mp, inputs, targets, w_in, w_out, teach_in, teach_out):
    in_scale = 1.0 / math.sqrt(inputs.shape[1] * mp)
    out_scale = 1.0 / math.sqrt(w_out.shape[0] * dp)
    tokens, ff = inputs.shape[0] * dp, w_in.shape[1]
    g, h, s, part, gs, w_in, w_out, teach_out = forward(
        dp // 4, in_scale, out_scale, inputs, targets, w_in, w_out, teach_out
    )
    other = lax.ppermute(part, "mp", [(0, 1), (1, 0)])
    grad_out, new_out = update(
        out_kernel, "update_out", out_scale, 128, 512, (), tokens,
        h, s, w_out, teach_out,
    )
    grad_in, new_in = update(
        in_kernel, "update_in", in_scale, 384, 256, (pltpu.VMEM((tokens, ff), BF16),), tokens,
        g, part, other, gs, w_in, teach_in,
    )
    return grad_in, grad_out, new_in, new_out


def plain_shards(dp, mp, inputs, targets, w_in, w_out, teach_in, teach_out):
    in_scale = 1.0 / math.sqrt(inputs.shape[1] * mp)
    out_scale = 1.0 / math.sqrt(w_out.shape[0] * dp)
    gathered = lax.all_gather(inputs, "dp", axis=0, tiled=True)
    preact = lax.psum(jnp.dot(gathered, w_in, preferred_element_type=F32) * in_scale, "mp")
    cdf = normal_cdf(preact)
    hidden = (preact * cdf).astype(BF16)
    summed = lax.psum_scatter(
        jnp.dot(hidden, w_out, preferred_element_type=F32) * out_scale,
        "dp", scatter_dimension=0, tiled=True,
    )
    own = (inputs.astype(F32) + summed - targets.astype(F32)).astype(BF16)
    slope = lax.all_gather(own, "dp", axis=0, tiled=True)
    part = jnp.einsum("td,fd->tf", slope, w_out, preferred_element_type=F32) * out_scale
    hidden_slope = lax.psum(part.astype(BF16), "mp").astype(F32)
    pre_slope = (hidden_slope * gelu_slope(preact, cdf)).astype(BF16)
    g_out = jnp.einsum("tf,td->fd", hidden, slope, preferred_element_type=F32) * out_scale
    g_in = jnp.einsum("td,tf->df", gathered, pre_slope, preferred_element_type=F32) * in_scale
    new_in = blended(teach_in, w_in, g_in)
    new_out = blended(teach_out, w_out, g_out)
    return g_in.astype(BF16), g_out.astype(BF16), new_in, new_out


def solution(mesh):
    dp, mp = mesh.shape["dp"], mesh.shape["mp"]
    body = shards if mp == 2 and dp == 16 else plain_shards
    return jax.shard_map(
        functools.partial(body, dp, mp),
        mesh=mesh,
        in_specs=(
            P("dp", "mp"),
            P("dp", "mp"),
            P("mp", "dp"),
            P("dp", "mp"),
            P("mp", "dp"),
            P("dp", "mp"),
        ),
        out_specs=(P("mp", "dp"), P("dp", "mp"), P("mp", "dp"), P("dp", "mp")),
        check_vma=False,
    )
```

```python
import functools
import math

import jax
import jax.numpy as jnp
from jax import lax
from jax.experimental import pallas as pl
from jax.experimental.pallas import tpu as pltpu
from jax.sharding import PartitionSpec as P

decay_rate = 0.99
step_size = 0.5
MESH = pl.DeviceIdType.MESH
F32 = jnp.float32
BF16 = jnp.bfloat16
MIB = 1024 * 1024


def normal_cdf(value):
    return 0.5 * (1.0 + lax.erf(value * (1.0 / math.sqrt(2.0))))


def gelu_slope(value, cdf):
    return cdf + value * jnp.exp(-0.5 * value * value) * (1.0 / math.sqrt(2.0 * math.pi))


def blended(teach, weight, grad):
    return decay_rate * teach + (1.0 - decay_rate) * (weight.astype(F32) - step_size * grad)


def forward_kernel(
    nz, in_scale, out_scale,
    x_hbm, t_hbm, w_in_hbm, w_out_hbm, teach_out_hbm,
    g, h, s, part, pre, w_in, w_out, teach_out,
    t_own, pre_send, pre_recv, acc, own,
    c_out, c_in, x_out, x_in, z_out, z_in,
    w_sem,
    ag_recv, ag_zs, ag_xs, ag_cs,
    sg_recv, sg_zs, sg_xs, sg_cs,
    y_s, y_r, c_s, c_r, x_s, x_r, z_s, z_r,
):
    rows, feats = t_own.shape
    ff = w_in.shape[1]
    group = 4 * rows
    me = lax.axis_index("dp")
    my = lax.axis_index("mp")
    z, xc = me // 4, me % 4
    x, c = xc // 2, xc % 2
    ox, oc = 1 - x, 1 - c
    mine = pl.ds(pl.multiple_of(me * rows, rows), rows)

    def index(zi, xi, ci):
        return (zi * 2 + xi) * 2 + ci

    def z_of(k):
        return ((z // 2 + k // 2) % (nz // 2)) * 2 + (z % 2 + k % 2) % 2

    loads = [
        pltpu.make_async_copy(src, dst, w_sem.at[i])
        for i, (src, dst) in enumerate((
            (x_hbm, g.at[mine, :]), (t_hbm, t_own), (w_in_hbm, w_in),
            (w_out_hbm, w_out), (teach_out_hbm, teach_out),
        ))
    ]
    for load in loads[:3]:
        load.start()

    barrier = pltpu.get_barrier_semaphore()
    for k in range(1, nz):
        pl.semaphore_signal(barrier, inc=1, device_id={"dp": index(z_of(k), x, c)}, device_id_type=MESH)
    pl.semaphore_signal(barrier, inc=1, device_id={"dp": index(z, ox, c)}, device_id_type=MESH)
    pl.semaphore_signal(barrier, inc=1, device_id={"dp": index(z, x, oc)}, device_id_type=MESH)
    pl.semaphore_signal(barrier, inc=1, device_id={"mp": 1 - my}, device_id_type=MESH)
    pl.semaphore_wait(barrier, nz + 2)

    def send(src, dst, ssem, rsem, to):
        return pltpu.make_async_remote_copy(
            src_ref=src, dst_ref=dst, send_sem=ssem, recv_sem=rsem,
            device_id=to, device_id_type=MESH,
        )

    pending = []

    def go(copy):
        copy.start()
        pending.append(copy)

    def gather(buf, recv, zs, xs, cs):
        def shard(o):
            return buf.at[pl.ds(pl.multiple_of(o * rows, rows), rows), :]

        def move(o, ssem, to):
            return send(shard(o), shard(o), ssem, recv.at[o], {"dp": to})

        to_x, to_c = index(z, ox, c), index(z, x, oc)

        def begin():
            go(move(me, xs.at[0], to_x))
            for k in range(1, nz):
                go(move(me, zs.at[k], index(z_of(k), x, c)))
            go(move(me, cs.at[0], to_c))

        def z_arrive(k):
            o = index(z_of(k), x, c)
            move(o, zs.at[k], to_c).wait_recv()
            go(move(o, xs.at[k], to_x))
            go(move(o, cs.at[k], to_c))

        def x_arrive(k):
            o = index(z_of(k), ox, c)
            move(o, xs.at[k], to_c).wait_recv()
            go(move(o, cs.at[nz + k], to_c))

        def c_arrive(k):
            for xi in (x, ox):
                move(index(z_of(k), xi, oc), cs.at[k], to_c).wait_recv()

        return begin, z_arrive, x_arrive, c_arrive

    def group_rows(k):
        return pl.ds(pl.multiple_of(z_of(k) * group, group), group)

    begin, z_arrive, x_arrive, c_arrive = gather(g, ag_recv, ag_zs, ag_xs, ag_cs)
    loads[0].wait()
    begin()
    for load in loads[3:]:
        load.start()

    def pre_step(k):
        x_arrive(k)
        c_arrive(k)
        if k == 0:
            loads[2].wait()
        at = group_rows(k)
        tile = min(512, ff)

        @pl.loop(0, ff // tile)
        def _(i):
            cols = pl.ds(pl.multiple_of(i * tile, tile), tile)
            value = jnp.dot(g[at, :], w_in[:, cols], preferred_element_type=F32) * in_scale
            pre[at, cols] = value
            pre_send[at, cols] = value.astype(BF16)

        go(send(pre_send.at[at, :], pre_recv.at[at, :], y_s.at[k], y_r.at[k], {"mp": 1 - my}))

    def out_step(k):
        at = group_rows(k)
        send(pre_send.at[at, :], pre_recv.at[at, :], y_s.at[k], y_r.at[k], {"mp": 1 - my}).wait_recv()
        tile = 256

        @pl.loop(0, ff // tile)
        def _(i):
            cols = pl.ds(pl.multiple_of(i * tile, tile), tile)
            value = pre[at, cols] + pre_recv[at, cols].astype(F32)
            cdf = normal_cdf(value)
            h[at, cols] = (value * cdf).astype(BF16)
            pre[at, cols] = gelu_slope(value, cdf)

        if k == 0:
            loads[3].wait()

        wide = 1024 if feats % 1024 == 0 else 256

        @pl.loop(0, feats // wide)
        def _(i):
            cols = pl.ds(pl.multiple_of(i * wide, wide), wide)
            acc[at, cols] = jnp.dot(h[at, :], w_out[:, cols], preferred_element_type=F32) * out_scale

        for xi in range(2):
            src = pl.ds(pl.multiple_of(index(z_of(k), xi, oc) * rows, rows), rows)
            c_out[k, pl.ds(xi * rows, rows), :] = acc[src, :].astype(BF16)
        go(send(c_out.at[k], c_in.at[k], c_s.at[k], c_r.at[k], {"dp": index(z, x, oc)}))

    def core_step(k):
        send(c_out.at[k], c_in.at[k], c_s.at[k], c_r.at[k], {"dp": index(z, x, oc)}).wait_recv()

        def total(xi):
            src = pl.ds(pl.multiple_of(index(z_of(k), xi, c) * rows, rows), rows)
            return acc[src, :] + c_in[k, pl.ds(pl.multiple_of(xi * rows, rows), rows), :].astype(F32)

        x_out[k] = total(ox).astype(BF16)
        go(send(x_out.at[k], x_in.at[k], x_s.at[k], x_r.at[k], {"dp": index(z, ox, c)}))
        own[k] = total(x)

    def x_step(k):
        send(x_out.at[k], x_in.at[k], x_s.at[k], x_r.at[k], {"dp": index(z, ox, c)}).wait_recv()
        value = own[k] + x_in[k].astype(F32)
        if k == 0:
            own[k] = value
        else:
            z_out[k] = value.astype(BF16)
            go(send(z_out.at[k], z_in.at[z], z_s.at[k], z_r.at[z], {"dp": index(z_of(k), x, c)}))

    z_arrive(1)
    pre_step(0)
    pre_step(1)
    for k in range(2, nz):
        z_arrive(k)
    for k in range(nz):
        out_step(k)
        if k + 2 < nz:
            pre_step(k + 2)
        if k > 0:
            x_step(k - 1)
        core_step(k)
    x_step(nz - 1)

    begin, z_arrive, x_arrive, c_arrive = gather(s, sg_recv, sg_zs, sg_xs, sg_cs)
    loads[1].wait()
    summed = own[0]
    for k in range(1, nz):
        zi = z_of(k)
        send(z_out.at[k], z_in.at[zi], z_s.at[k], z_r.at[zi], {"dp": index(zi, x, c)}).wait_recv()
        summed += z_in[zi].astype(F32)
    slope = g[mine, :].astype(F32) + summed - t_own[...].astype(F32)
    s[mine, :] = slope.astype(BF16)
    begin()

    z_arrive(1)
    x_arrive(0)
    x_arrive(1)
    for k in range(2, nz):
        z_arrive(k)
    for k in range(2, nz):
        x_arrive(k)
    for k in range(nz):
        c_arrive(k)
    tile = min(512, ff)

    @pl.loop(0, ff // tile)
    def _(i):
        units = pl.ds(pl.multiple_of(i * tile, tile), tile)
        value = lax.dot_general(
            s[...], w_out[units, :], (((1,), (1,)), ((), ())), preferred_element_type=F32
        )
        part[:, units] = (value * out_scale).astype(BF16)

    for copy in pending:
        copy.wait_send()
    for load in loads[4:]:
        load.wait()


def forward(nz, in_scale, out_scale, inputs, targets, w_in, w_out, teach_out):
    rows, feats = inputs.shape
    ff = w_in.shape[1]
    tokens = rows * nz * 4
    dma = pltpu.SemaphoreType.DMA
    vmem = pl.BlockSpec(memory_space=pltpu.VMEM)
    return pl.pallas_call(
        functools.partial(forward_kernel, nz, in_scale, out_scale),
        out_shape=(
            pltpu.VMEM((tokens, feats), BF16),
            pltpu.VMEM((tokens, ff), BF16),
            pltpu.VMEM((tokens, feats), BF16),
            pltpu.VMEM((tokens, ff), BF16),
            pltpu.VMEM((tokens, ff), F32),
            pltpu.VMEM((feats, ff), BF16),
            pltpu.VMEM((ff, feats), BF16),
            pltpu.VMEM((ff, feats), F32),
        ),
        in_specs=[pl.BlockSpec(memory_space=pltpu.HBM)] * 5,
        out_specs=(vmem,) * 8,
        scratch_shapes=[
            pltpu.VMEM((rows, feats), BF16),
            pltpu.VMEM((tokens, ff), BF16),
            pltpu.VMEM((tokens, ff), BF16),
            pltpu.VMEM((tokens, feats), F32),
            pltpu.VMEM((nz, rows, feats), F32),
            pltpu.VMEM((nz, 2 * rows, feats), BF16),
            pltpu.VMEM((nz, 2 * rows, feats), BF16),
            pltpu.VMEM((nz, rows, feats), BF16),
            pltpu.VMEM((nz, rows, feats), BF16),
            pltpu.VMEM((nz, rows, feats), BF16),
            pltpu.VMEM((nz, rows, feats), BF16),
            dma((5,)),
            dma((4 * nz,)), dma((nz,)), dma((nz,)), dma((2 * nz,)),
            dma((4 * nz,)), dma((nz,)), dma((nz,)), dma((2 * nz,)),
            dma((nz,)), dma((nz,)),
            dma((nz,)), dma((nz,)), dma((nz,)), dma((nz,)), dma((nz,)), dma((nz,)),
        ],
        compiler_params=pltpu.CompilerParams(
            collective_id=0, has_side_effects=True, vmem_limit_bytes=12 * MIB
        ),
        cost_estimate=pl.CostEstimate(
            flops=6 * tokens * feats * ff, bytes_accessed=12 * feats * ff, transcendentals=0
        ),
        name="forward",
    )(*[
        pltpu.with_memory_space_constraint(x, pltpu.HBM)
        for x in (inputs, targets, w_in, w_out, teach_out)
    ])


def write_update(scale, tile, cols_tile, left, right, w, t, grad_hbm, new_hbm, grads, news, turned, sems):
    count, width = w.shape
    slots = grads.shape[0]
    steps = count // tile

    def writes(i, slot):
        at = pl.ds(pl.multiple_of(i * tile, tile), tile)
        return (
            pltpu.make_async_copy(grads.at[slot], grad_hbm.at[at, :], sems.at[0, slot]),
            pltpu.make_async_copy(news.at[slot], new_hbm.at[at, :], sems.at[1, slot]),
        )

    @pl.loop(0, steps)
    def _(i):
        slot = i % slots

        @pl.when(i >= slots)
        def _():
            for copy in writes(i - slots, slot):
                copy.wait()

        at = pl.ds(pl.multiple_of(i * tile, tile), tile)
        turned[...] = left[:, at].T
        for n in range(0, width, cols_tile):
            cols = slice(n, n + cols_tile)
            grad = jnp.dot(turned[...], right[:, cols], preferred_element_type=F32) * scale
            grads[slot, :, cols] = grad.astype(BF16)
            news[slot, :, cols] = blended(t[at, cols], w[at, cols], grad)
        for copy in writes(i, slot):
            copy.start()

    for i in range(max(steps - slots, 0), steps):
        for copy in writes(i, i % slots):
            copy.wait()


def out_kernel(scale, tile, cols, h, s, w, t, *rest):
    write_update(scale, tile, cols, h, s, w, t, *rest)


def in_kernel(scale, tile, cols, g, part, other, gs, w, t, grad_hbm, new_hbm, grads, news, turned, sems, pre_slope):
    total = part[...].astype(F32) + other[...].astype(F32)
    pre_slope[...] = (total * gs[...]).astype(BF16)
    write_update(scale, tile, cols, g, pre_slope, w, t, grad_hbm, new_hbm, grads, news, turned, sems)


def update(kernel, name, scale, tile, cols, extra, tokens, *operands):
    count, width = operands[-1].shape
    slots = 3
    vmem = pl.BlockSpec(memory_space=pltpu.VMEM)
    anywhere = pl.BlockSpec(memory_space=pl.ANY)
    return pl.pallas_call(
        functools.partial(kernel, scale, tile, cols),
        out_shape=(
            jax.ShapeDtypeStruct((count, width), BF16),
            jax.ShapeDtypeStruct((count, width), F32),
        ),
        in_specs=[vmem] * len(operands),
        out_specs=(anywhere, anywhere),
        scratch_shapes=[
            pltpu.VMEM((slots, tile, width), BF16),
            pltpu.VMEM((slots, tile, width), F32),
            pltpu.VMEM((tile, tokens), BF16),
            pltpu.SemaphoreType.DMA((2, slots)),
            *extra,
        ],
        compiler_params=pltpu.CompilerParams(vmem_limit_bytes=12 * MIB),
        cost_estimate=pl.CostEstimate(
            flops=2 * tokens * count * width, bytes_accessed=12 * count * width, transcendentals=0
        ),
        name=name,
    )(*[pltpu.with_memory_space_constraint(x, pltpu.VMEM) for x in operands])


def shards(dp, mp, inputs, targets, w_in, w_out, teach_in, teach_out):
    in_scale = 1.0 / math.sqrt(inputs.shape[1] * mp)
    out_scale = 1.0 / math.sqrt(w_out.shape[0] * dp)
    tokens, ff = inputs.shape[0] * dp, w_in.shape[1]
    g, h, s, part, gs, w_in, w_out, teach_out = forward(
        dp // 4, in_scale, out_scale, inputs, targets, w_in, w_out, teach_out
    )
    other = lax.ppermute(part, "mp", [(0, 1), (1, 0)])
    grad_out, new_out = update(
        out_kernel, "update_out", out_scale, 128, 256, (), tokens,
        h, s, w_out, teach_out,
    )
    grad_in, new_in = update(
        in_kernel, "update_in", in_scale, 384, 256, (pltpu.VMEM((tokens, ff), BF16),), tokens,
        g, part, other, gs, w_in, teach_in,
    )
    return grad_in, grad_out, new_in, new_out


def plain_shards(dp, mp, inputs, targets, w_in, w_out, teach_in, teach_out):
    in_scale = 1.0 / math.sqrt(inputs.shape[1] * mp)
    out_scale = 1.0 / math.sqrt(w_out.shape[0] * dp)
    gathered = lax.all_gather(inputs, "dp", axis=0, tiled=True)
    preact = lax.psum(jnp.dot(gathered, w_in, preferred_element_type=F32) * in_scale, "mp")
    cdf = normal_cdf(preact)
    hidden = (preact * cdf).astype(BF16)
    summed = lax.psum_scatter(
        jnp.dot(hidden, w_out, preferred_element_type=F32) * out_scale,
        "dp", scatter_dimension=0, tiled=True,
    )
    own = (inputs.astype(F32) + summed - targets.astype(F32)).astype(BF16)
    slope = lax.all_gather(own, "dp", axis=0, tiled=True)
    part = jnp.einsum("td,fd->tf", slope, w_out, preferred_element_type=F32) * out_scale
    hidden_slope = lax.psum(part.astype(BF16), "mp").astype(F32)
    pre_slope = (hidden_slope * gelu_slope(preact, cdf)).astype(BF16)
    g_out = jnp.einsum("tf,td->fd", hidden, slope, preferred_element_type=F32) * out_scale
    g_in = jnp.einsum("td,tf->df", gathered, pre_slope, preferred_element_type=F32) * in_scale
    new_in = blended(teach_in, w_in, g_in)
    new_out = blended(teach_out, w_out, g_out)
    return g_in.astype(BF16), g_out.astype(BF16), new_in, new_out


def solution(mesh):
    dp, mp = mesh.shape["dp"], mesh.shape["mp"]
    body = shards if mp == 2 and dp == 16 else plain_shards
    return jax.shard_map(
        functools.partial(body, dp, mp),
        mesh=mesh,
        in_specs=(
            P("dp", "mp"),
            P("dp", "mp"),
            P("mp", "dp"),
            P("dp", "mp"),
            P("mp", "dp"),
            P("dp", "mp"),
        ),
        out_specs=(P("mp", "dp"), P("dp", "mp"), P("mp", "dp"), P("dp", "mp")),
        check_vma=False,
    )
```

```python
import functools
import math

import jax
import jax.numpy as jnp
from jax import lax
from jax.experimental import pallas as pl
from jax.experimental.pallas import tpu as pltpu
from jax.sharding import PartitionSpec as P

decay_rate = 0.99
step_size = 0.5
MESH = pl.DeviceIdType.MESH
F32 = jnp.float32
BF16 = jnp.bfloat16
MIB = 1024 * 1024


def normal_cdf(value):
    return 0.5 * (1.0 + lax.erf(value * (1.0 / math.sqrt(2.0))))


def gelu_slope(value, cdf):
    return cdf + value * jnp.exp(-0.5 * value * value) * (1.0 / math.sqrt(2.0 * math.pi))


def blended(teach, weight, grad):
    return decay_rate * teach + (1.0 - decay_rate) * (weight.astype(F32) - step_size * grad)


def forward_kernel(
    nz, in_scale, out_scale,
    x_hbm, t_hbm, w_in_hbm, w_out_hbm, teach_out_hbm,
    g, h, s, near, near_in, far, pre, w_in, w_out, teach_out,
    t_own, pre_send, pre_recv, acc, own,
    c_out, c_in, x_out, x_in, z_out, z_in,
    w_sem,
    ag_recv, ag_zs, ag_xs, ag_cs,
    sg_recv, sg_zs, sg_xs, sg_cs,
    y_s, y_r, c_s, c_r, x_s, x_r, z_s, z_r, n_s, n_r,
):
    rows, feats = t_own.shape
    ff = w_in.shape[1]
    group = 4 * rows
    me = lax.axis_index("dp")
    my = lax.axis_index("mp")
    z, xc = me // 4, me % 4
    x, c = xc // 2, xc % 2
    ox, oc = 1 - x, 1 - c
    mine = pl.ds(pl.multiple_of(me * rows, rows), rows)

    def index(zi, xi, ci):
        return (zi * 2 + xi) * 2 + ci

    def z_of(k):
        return ((z // 2 + k // 2) % (nz // 2)) * 2 + (z % 2 + k % 2) % 2

    loads = [
        pltpu.make_async_copy(src, dst, w_sem.at[i])
        for i, (src, dst) in enumerate((
            (x_hbm, g.at[mine, :]), (t_hbm, t_own), (w_in_hbm, w_in),
            (w_out_hbm, w_out), (teach_out_hbm, teach_out),
        ))
    ]
    for load in loads[:3]:
        load.start()

    barrier = pltpu.get_barrier_semaphore()
    for k in range(1, nz):
        pl.semaphore_signal(barrier, inc=1, device_id={"dp": index(z_of(k), x, c)}, device_id_type=MESH)
    pl.semaphore_signal(barrier, inc=1, device_id={"dp": index(z, ox, c)}, device_id_type=MESH)
    pl.semaphore_signal(barrier, inc=1, device_id={"dp": index(z, x, oc)}, device_id_type=MESH)
    pl.semaphore_signal(barrier, inc=1, device_id={"mp": 1 - my}, device_id_type=MESH)
    pl.semaphore_wait(barrier, nz + 2)

    def send(src, dst, ssem, rsem, to):
        return pltpu.make_async_remote_copy(
            src_ref=src, dst_ref=dst, send_sem=ssem, recv_sem=rsem,
            device_id=to, device_id_type=MESH,
        )

    pending = []

    def go(copy):
        copy.start()
        pending.append(copy)

    def gather(buf, recv, zs, xs, cs):
        def shard(o):
            return buf.at[pl.ds(pl.multiple_of(o * rows, rows), rows), :]

        def move(o, ssem, to):
            return send(shard(o), shard(o), ssem, recv.at[o], {"dp": to})

        to_x, to_c = index(z, ox, c), index(z, x, oc)

        def begin():
            go(move(me, xs.at[0], to_x))
            for k in range(1, nz):
                go(move(me, zs.at[k], index(z_of(k), x, c)))
            go(move(me, cs.at[0], to_c))

        def z_arrive(k):
            o = index(z_of(k), x, c)
            move(o, zs.at[k], to_c).wait_recv()
            go(move(o, xs.at[k], to_x))
            go(move(o, cs.at[k], to_c))

        def x_arrive(k):
            o = index(z_of(k), ox, c)
            move(o, xs.at[k], to_c).wait_recv()
            go(move(o, cs.at[nz + k], to_c))

        def c_arrive(k):
            for xi in (x, ox):
                move(index(z_of(k), xi, oc), cs.at[k], to_c).wait_recv()

        return begin, z_arrive, x_arrive, c_arrive

    def group_rows(k):
        return pl.ds(pl.multiple_of(z_of(k) * group, group), group)

    begin, z_arrive, x_arrive, c_arrive = gather(g, ag_recv, ag_zs, ag_xs, ag_cs)
    loads[0].wait()
    begin()
    for load in loads[3:]:
        load.start()

    def pre_step(k):
        x_arrive(k)
        c_arrive(k)
        if k == 0:
            loads[2].wait()
        at = group_rows(k)
        tile = min(512, ff)

        @pl.loop(0, ff // tile)
        def _(i):
            cols = pl.ds(pl.multiple_of(i * tile, tile), tile)
            value = jnp.dot(g[at, :], w_in[:, cols], preferred_element_type=F32) * in_scale
            pre[at, cols] = value
            pre_send[at, cols] = value.astype(BF16)

        go(send(pre_send.at[at, :], pre_recv.at[at, :], y_s.at[k], y_r.at[k], {"mp": 1 - my}))

    def out_step(k):
        at = group_rows(k)
        send(pre_send.at[at, :], pre_recv.at[at, :], y_s.at[k], y_r.at[k], {"mp": 1 - my}).wait_recv()
        tile = 256

        @pl.loop(0, ff // tile)
        def _(i):
            cols = pl.ds(pl.multiple_of(i * tile, tile), tile)
            value = pre[at, cols] + pre_recv[at, cols].astype(F32)
            cdf = normal_cdf(value)
            h[at, cols] = (value * cdf).astype(BF16)
            pre[at, cols] = gelu_slope(value, cdf)

        if k == 0:
            loads[3].wait()

        wide = 1024 if feats % 1024 == 0 else 256

        @pl.loop(0, feats // wide)
        def _(i):
            cols = pl.ds(pl.multiple_of(i * wide, wide), wide)
            acc[at, cols] = jnp.dot(h[at, :], w_out[:, cols], preferred_element_type=F32) * out_scale

        for xi in range(2):
            src = pl.ds(pl.multiple_of(index(z_of(k), xi, oc) * rows, rows), rows)
            c_out[k, pl.ds(xi * rows, rows), :] = acc[src, :].astype(BF16)
        go(send(c_out.at[k], c_in.at[k], c_s.at[k], c_r.at[k], {"dp": index(z, x, oc)}))

    def core_step(k):
        send(c_out.at[k], c_in.at[k], c_s.at[k], c_r.at[k], {"dp": index(z, x, oc)}).wait_recv()

        def total(xi):
            src = pl.ds(pl.multiple_of(index(z_of(k), xi, c) * rows, rows), rows)
            return acc[src, :] + c_in[k, pl.ds(pl.multiple_of(xi * rows, rows), rows), :].astype(F32)

        x_out[k] = total(ox).astype(BF16)
        go(send(x_out.at[k], x_in.at[k], x_s.at[k], x_r.at[k], {"dp": index(z, ox, c)}))
        own[k] = total(x)

    def x_step(k):
        send(x_out.at[k], x_in.at[k], x_s.at[k], x_r.at[k], {"dp": index(z, ox, c)}).wait_recv()
        value = own[k] + x_in[k].astype(F32)
        if k == 0:
            own[k] = value
        else:
            z_out[k] = value.astype(BF16)
            go(send(z_out.at[k], z_in.at[z], z_s.at[k], z_r.at[z], {"dp": index(z_of(k), x, c)}))

    z_arrive(1)
    pre_step(0)
    pre_step(1)
    for k in range(2, nz):
        z_arrive(k)
    for k in range(nz):
        out_step(k)
        if k + 2 < nz:
            pre_step(k + 2)
        if k > 0:
            x_step(k - 1)
        core_step(k)
    x_step(nz - 1)

    begin, z_arrive, x_arrive, c_arrive = gather(s, sg_recv, sg_zs, sg_xs, sg_cs)
    loads[1].wait()
    summed = own[0]
    for k in range(1, nz):
        zi = z_of(k)
        send(z_out.at[k], z_in.at[zi], z_s.at[k], z_r.at[zi], {"dp": index(zi, x, c)}).wait_recv()
        summed += z_in[zi].astype(F32)
    slope = g[mine, :].astype(F32) + summed - t_own[...].astype(F32)
    s[mine, :] = slope.astype(BF16)
    begin()

    half = 2 * group
    tile = min(512, ff)

    def slope_step(j, out):
        at = pl.ds(pl.multiple_of((z_of(2 * j) // 2) * half, half), half)

        @pl.loop(0, ff // tile)
        def _(i):
            units = pl.ds(pl.multiple_of(i * tile, tile), tile)
            value = lax.dot_general(
                s[at, :], w_out[units, :], (((1,), (1,)), ((), ())), preferred_element_type=F32
            )
            out[:, units] = (value * out_scale).astype(BF16)

    z_arrive(1)
    x_arrive(0)
    x_arrive(1)
    c_arrive(0)
    c_arrive(1)
    slope_step(0, near)
    swap = send(near, near_in, n_s.at[0], n_r.at[0], {"mp": 1 - my})
    go(swap)
    for k in range(2, nz):
        z_arrive(k)
    for k in range(2, nz):
        x_arrive(k)
    for k in range(2, nz):
        c_arrive(k)
    slope_step(1, far)
    swap.wait_recv()

    for copy in pending:
        copy.wait_send()
    for load in loads[4:]:
        load.wait()


def forward(nz, in_scale, out_scale, inputs, targets, w_in, w_out, teach_out):
    rows, feats = inputs.shape
    ff = w_in.shape[1]
    tokens = rows * nz * 4
    dma = pltpu.SemaphoreType.DMA
    vmem = pl.BlockSpec(memory_space=pltpu.VMEM)
    return pl.pallas_call(
        functools.partial(forward_kernel, nz, in_scale, out_scale),
        out_shape=(
            pltpu.VMEM((tokens, feats), BF16),
            pltpu.VMEM((tokens, ff), BF16),
            pltpu.VMEM((tokens, feats), BF16),
            pltpu.VMEM((tokens // 2, ff), BF16),
            pltpu.VMEM((tokens // 2, ff), BF16),
            pltpu.VMEM((tokens // 2, ff), BF16),
            pltpu.VMEM((tokens, ff), F32),
            pltpu.VMEM((feats, ff), BF16),
            pltpu.VMEM((ff, feats), BF16),
            pltpu.VMEM((ff, feats), F32),
        ),
        in_specs=[pl.BlockSpec(memory_space=pltpu.HBM)] * 5,
        out_specs=(vmem,) * 10,
        scratch_shapes=[
            pltpu.VMEM((rows, feats), BF16),
            pltpu.VMEM((tokens, ff), BF16),
            pltpu.VMEM((tokens, ff), BF16),
            pltpu.VMEM((tokens, feats), F32),
            pltpu.VMEM((nz, rows, feats), F32),
            pltpu.VMEM((nz, 2 * rows, feats), BF16),
            pltpu.VMEM((nz, 2 * rows, feats), BF16),
            pltpu.VMEM((nz, rows, feats), BF16),
            pltpu.VMEM((nz, rows, feats), BF16),
            pltpu.VMEM((nz, rows, feats), BF16),
            pltpu.VMEM((nz, rows, feats), BF16),
            dma((5,)),
            dma((4 * nz,)), dma((nz,)), dma((nz,)), dma((2 * nz,)),
            dma((4 * nz,)), dma((nz,)), dma((nz,)), dma((2 * nz,)),
            dma((nz,)), dma((nz,)),
            dma((nz,)), dma((nz,)), dma((nz,)), dma((nz,)), dma((nz,)), dma((nz,)),
            dma((1,)), dma((1,)),
        ],
        compiler_params=pltpu.CompilerParams(
            collective_id=0, has_side_effects=True, vmem_limit_bytes=12 * MIB
        ),
        cost_estimate=pl.CostEstimate(
            flops=6 * tokens * feats * ff, bytes_accessed=12 * feats * ff, transcendentals=0
        ),
        name="forward",
    )(*[
        pltpu.with_memory_space_constraint(x, pltpu.HBM)
        for x in (inputs, targets, w_in, w_out, teach_out)
    ])


def write_update(scale, tile, cols_tile, left, right, w, t, grad_hbm, new_hbm, grads, news, turned, sems):
    count, width = w.shape
    slots = grads.shape[0]
    steps = count // tile

    def writes(i, slot):
        at = pl.ds(pl.multiple_of(i * tile, tile), tile)
        return (
            pltpu.make_async_copy(grads.at[slot], grad_hbm.at[at, :], sems.at[0, slot]),
            pltpu.make_async_copy(news.at[slot], new_hbm.at[at, :], sems.at[1, slot]),
        )

    @pl.loop(0, steps)
    def _(i):
        slot = i % slots

        @pl.when(i >= slots)
        def _():
            for copy in writes(i - slots, slot):
                copy.wait()

        at = pl.ds(pl.multiple_of(i * tile, tile), tile)
        turned[...] = left[:, at].T
        for n in range(0, width, cols_tile):
            cols = slice(n, n + cols_tile)
            grad = jnp.dot(turned[...], right[:, cols], preferred_element_type=F32) * scale
            grads[slot, :, cols] = grad.astype(BF16)
            news[slot, :, cols] = blended(t[at, cols], w[at, cols], grad)
        for copy in writes(i, slot):
            copy.start()

    for i in range(max(steps - slots, 0), steps):
        for copy in writes(i, i % slots):
            copy.wait()


def out_kernel(scale, tile, cols, h, s, w, t, *rest):
    write_update(scale, tile, cols, h, s, w, t, *rest)


def in_kernel(scale, tile, cols, g, near, near_in, far, far_in, gs, w, t, grad_hbm, new_hbm, grads, news, turned, sems, pre_slope):
    half = near.shape[0]
    side = lax.axis_index("dp") // 8
    for here, there, first in ((near, near_in, side), (far, far_in, 1 - side)):
        at = pl.ds(pl.multiple_of(first * half, half), half)
        total = here[...].astype(F32) + there[...].astype(F32)
        pre_slope[at, :] = (total * gs[at, :]).astype(BF16)
    write_update(scale, tile, cols, g, pre_slope, w, t, grad_hbm, new_hbm, grads, news, turned, sems)


def update(kernel, name, scale, tile, cols, extra, tokens, *operands):
    count, width = operands[-1].shape
    slots = 3
    vmem = pl.BlockSpec(memory_space=pltpu.VMEM)
    anywhere = pl.BlockSpec(memory_space=pl.ANY)
    return pl.pallas_call(
        functools.partial(kernel, scale, tile, cols),
        out_shape=(
            jax.ShapeDtypeStruct((count, width), BF16),
            jax.ShapeDtypeStruct((count, width), F32),
        ),
        in_specs=[vmem] * len(operands),
        out_specs=(anywhere, anywhere),
        scratch_shapes=[
            pltpu.VMEM((slots, tile, width), BF16),
            pltpu.VMEM((slots, tile, width), F32),
            pltpu.VMEM((tile, tokens), BF16),
            pltpu.SemaphoreType.DMA((2, slots)),
            *extra,
        ],
        compiler_params=pltpu.CompilerParams(vmem_limit_bytes=12 * MIB),
        cost_estimate=pl.CostEstimate(
            flops=2 * tokens * count * width, bytes_accessed=12 * count * width, transcendentals=0
        ),
        name=name,
    )(*[pltpu.with_memory_space_constraint(x, pltpu.VMEM) for x in operands])


def shards(dp, mp, inputs, targets, w_in, w_out, teach_in, teach_out):
    in_scale = 1.0 / math.sqrt(inputs.shape[1] * mp)
    out_scale = 1.0 / math.sqrt(w_out.shape[0] * dp)
    tokens, ff = inputs.shape[0] * dp, w_in.shape[1]
    g, h, s, near, near_in, far, gs, w_in, w_out, teach_out = forward(
        dp // 4, in_scale, out_scale, inputs, targets, w_in, w_out, teach_out
    )
    far_in = lax.ppermute(far, "mp", [(0, 1), (1, 0)])
    grad_out, new_out = update(
        out_kernel, "update_out", out_scale, 128, 256, (), tokens,
        h, s, w_out, teach_out,
    )
    grad_in, new_in = update(
        in_kernel, "update_in", in_scale, 384, 256, (pltpu.VMEM((tokens, ff), BF16),), tokens,
        g, near, near_in, far, far_in, gs, w_in, teach_in,
    )
    return grad_in, grad_out, new_in, new_out


def plain_shards(dp, mp, inputs, targets, w_in, w_out, teach_in, teach_out):
    in_scale = 1.0 / math.sqrt(inputs.shape[1] * mp)
    out_scale = 1.0 / math.sqrt(w_out.shape[0] * dp)
    gathered = lax.all_gather(inputs, "dp", axis=0, tiled=True)
    preact = lax.psum(jnp.dot(gathered, w_in, preferred_element_type=F32) * in_scale, "mp")
    cdf = normal_cdf(preact)
    hidden = (preact * cdf).astype(BF16)
    summed = lax.psum_scatter(
        jnp.dot(hidden, w_out, preferred_element_type=F32) * out_scale,
        "dp", scatter_dimension=0, tiled=True,
    )
    own = (inputs.astype(F32) + summed - targets.astype(F32)).astype(BF16)
    slope = lax.all_gather(own, "dp", axis=0, tiled=True)
    part = jnp.einsum("td,fd->tf", slope, w_out, preferred_element_type=F32) * out_scale
    hidden_slope = lax.psum(part.astype(BF16), "mp").astype(F32)
    pre_slope = (hidden_slope * gelu_slope(preact, cdf)).astype(BF16)
    g_out = jnp.einsum("tf,td->fd", hidden, slope, preferred_element_type=F32) * out_scale
    g_in = jnp.einsum("td,tf->df", gathered, pre_slope, preferred_element_type=F32) * in_scale
    new_in = blended(teach_in, w_in, g_in)
    new_out = blended(teach_out, w_out, g_out)
    return g_in.astype(BF16), g_out.astype(BF16), new_in, new_out


def solution(mesh):
    dp, mp = mesh.shape["dp"], mesh.shape["mp"]
    body = shards if mp == 2 and dp == 16 else plain_shards
    return jax.shard_map(
        functools.partial(body, dp, mp),
        mesh=mesh,
        in_specs=(
            P("dp", "mp"),
            P("dp", "mp"),
            P("mp", "dp"),
            P("dp", "mp"),
            P("mp", "dp"),
            P("dp", "mp"),
        ),
        out_specs=(P("mp", "dp"), P("dp", "mp"), P("mp", "dp"), P("dp", "mp")),
        check_vma=False,
    )
```
